256 devices in a mesh: section: 4 (over x), dp: 64 (over z, y, core).
Axes of the slice: x: 4, y: 4, z: 8, core: 2. Of those that a mesh axis runs over, the one named last changes fastest.
Arguments:
- grads: bfloat16 [4, 64, 22, 288, 1024], P('section', 'dp'), may hold values from -6 to 6
- momentum: bfloat16 [4, 22, 294912], P('section', None, 'dp'), may hold values from -48 to 48
- weights: bfloat16 [4, 22, 294912], P('section', None, 'dp'), may hold values from -1.1953125 to 1.1953125
Outputs:
- new_weights: bfloat16 [4, 22, 294912], P('section', None, 'dp')
The draws below stay inside these ranges and needn't reach their ends.
All inputs are finite; a program needn't handle non-finite values.
Results may differ from the reference program's by a relative error of at most 0.02.
Values may be sent and summed in bfloat16 or wider, within the bound.
A program may use at most 128 MiB of HBM per device.

```python
import math
import jax
import jax.numpy as jnp
from jax import lax

R = 288
C = 1024
ITERS = 5
MS = 22
N_SECTION = 4
N_DP = 64


def strengthened(array, own_key, source, target, parts, factor):
    def block_of(position):
        return (jnp.arange(array.shape[position]) // (array.shape[position] // parts)).reshape((-1,) + (1,) * (array.ndim - 1 - position))

    one_side = jax.random.permutation(own_key, parts)[block_of(target)]
    other_side = (block_of(target) + parts // 2) % parts
    return jnp.where((block_of(source) == one_side) | (block_of(source) == other_side), factor * array, array)


def block_levels(stream_key, extent, split, least, largest):
    loudness, own = 1.0, jax.random.fold_in(stream_key, 6)
    for axis_at, parts in split:
        heights = jnp.exp(jax.random.uniform(jax.random.fold_in(own, axis_at), (parts,), jnp.float32, least / len(split), largest / len(split)))
        loudness = loudness * jnp.repeat(heights, extent[axis_at] // parts).reshape([-1 if axis == axis_at else 1 for axis in range(len(extent))])
    return loudness


def normal_values(rng, shape, deviation, reach, pieces=(), kind=jnp.bfloat16):
    loudness = block_levels(rng, shape, pieces, -0.22, 0.18) if pieces else 1.0
    array = jax.random.normal(rng, shape, jnp.float32) * deviation * loudness
    return jnp.minimum(jnp.maximum(array, -reach), reach).astype(kind)


def heavy_noise(own_key, extent, scale, limit, split, heavy, held_as=jnp.bfloat16):
    drawn = scale * jax.random.normal(own_key, extent, jnp.float32)
    if split:
        drawn = drawn * block_levels(own_key, extent, split, -0.22, 0.18)
    return jnp.clip(strengthened(drawn, jax.random.fold_in(own_key, 3), *heavy), -limit, limit).astype(held_as)


def setup_inputs(seed: int = 0) -> dict:
    seeds = jax.random.split(jax.random.key(seed), 4)
    grads = heavy_noise(seeds[0], (N_SECTION, N_DP, MS, R, C), 1.0, 6.0, ((0, 4), (1, 64)), (1, 3, 32, 2.75))
    momentum = normal_values(seeds[1], (N_SECTION, MS, R * C), 8.0, 48.0, ((0, 4), (2, 64)))
    weights = normal_values(seeds[2], (N_SECTION, MS, R * C), 0.2, 1.1953125, ((0, 4), (2, 64)))
    return dict(grads=grads, momentum=momentum, weights=weights)


QUINTIC_A = 3.4445
QUINTIC_B = -4.775
QUINTIC_C = 2.0315
MOMENTUM_DECAY = 0.95
LEARN_RATE = 0.5
DECAY_RATE = 0.1
EPSILON = 1e-07

def newton(current):
    for repeat_index in range(ITERS):
        gram_matrix = jnp.dot(current, current.T, preferred_element_type=jnp.float32).astype(jnp.bfloat16)
        square = jnp.dot(gram_matrix, gram_matrix, preferred_element_type=jnp.float32)
        polynomial = (QUINTIC_B * gram_matrix.astype(jnp.float32) + QUINTIC_C * square).astype(jnp.bfloat16)
        mixed = jnp.dot(polynomial, current, preferred_element_type=jnp.float32)
        current = (QUINTIC_A * current.astype(jnp.float32) + mixed).astype(jnp.bfloat16)
    return current

def reference(grads, momentum, weights):
    factor = 0.2 * math.sqrt(max(R, C))
    sections = []
    for section_index in range(N_SECTION):
        summed = lax.optimization_barrier(jnp.sum(grads[section_index], axis=0, dtype=jnp.float32))
        rounded = summed.astype(jnp.bfloat16).astype(jnp.float32)
        matrices_out = []
        for index in range(MS):
            stored = momentum[section_index, index].astype(jnp.float32).reshape(R, C)
            velocity = MOMENTUM_DECAY * stored + rounded[index]
            blended = rounded[index] + MOMENTUM_DECAY * velocity
            frobenius = jnp.sqrt(jnp.sum(blended * blended)) + EPSILON
            normalized = (blended / frobenius).astype(jnp.bfloat16)
            orthogonal = newton(normalized).astype(jnp.float32).reshape(-1)
            updated = weights[section_index, index].astype(jnp.float32) * (1.0 - LEARN_RATE * DECAY_RATE) - LEARN_RATE * factor * orthogonal
            matrices_out.append(updated.astype(jnp.bfloat16))
        sections.append(jnp.stack(matrices_out))
    return jnp.stack(sections)
```

```python
import math

import jax
import jax.numpy as jnp
from jax import lax
from jax.experimental import pallas as pl
from jax.experimental.pallas import tpu as pltpu
from jax.sharding import PartitionSpec as P

ITERS = 5
QUINTIC_A = 3.4445
QUINTIC_B = -4.775
QUINTIC_C = 2.0315
MOMENTUM_DECAY = 0.95
LEARN_RATE = 0.5
DECAY_RATE = 0.1
EPSILON = 1e-07

NZ, NY = 8, 4
MATRICES, HEIGHT, BREADTH = 22, 288, 1024
HALF = MATRICES // 2
GROUPS = 64
PORTION = HEIGHT * BREADTH // GROUPS
STRIPS = PORTION // 128
STRIP_ROWS = 48
WINDOW = 32
LOW = (0, 64, 128, 208)
COUNT = (64, 64, 80, 80)
MESH = pl.DeviceIdType.MESH
F32, BF16 = jnp.float32, jnp.bfloat16
Z_UP, Z_DOWN, Y_UP, Y_DOWN = range(4)


def place(dp):
    return dp // 8, lax.rem(dp // 2, NY), lax.rem(dp, 2)


def owner_z(j, c):
    return lax.rem(j + 3 * c, NZ)


def owner_y(j, c):
    return lax.rem(j + j // 8 + 2 * c, NY)


def owned(dp):
    z, y, c = place(dp)
    v = lax.rem(z + NZ - 3 * c, NZ)
    first = owner_y(v, c) == y
    second = jnp.logical_and(v < 3, owner_y(v + 8, c) == y)
    return jnp.minimum(jnp.where(first, v, v + 8), HALF - 1), jnp.logical_or(first, second)


def first_candidates(axis, d, z, y, c):
    if axis == 0:
        u = lax.rem(z + d + NZ - 3 * c, NZ)
        return [(u, None), (jnp.minimum(u + 8, HALF - 1), u < 3)]
    u = lax.rem(y + d + NY - 2 * c, NY)
    return [(u, None), (u + 4, None), (jnp.minimum(u + 7, HALF - 1), u >= 1)]


def guarded(valid, body):
    if valid is None:
        body()
    else:
        pl.when(valid)(body)


def roles(axis, d, half):
    n = NZ if axis == 0 else NY
    up = lambda e: 1 <= e < n // 2 or (e == n // 2 and half == 0)
    down = lambda e: n // 2 < e < n or (e == n // 2 and half == 1)
    receives = []
    if up(d + 1):
        receives.append(2 * axis)
    if down((d - 1) % n):
        receives.append(2 * axis + 1)
    sends = 2 * axis if up(d) else 2 * axis + 1 if down(d) else None
    return receives, sends


FIRST = (
    [(0, 4, 0), (0, 4, 1), (1, 2, 0), (1, 2, 1), (0, 3, 1), (0, 5, 0), (1, 1, 1), (1, 3, 0)]
    + [(0, 3, 0), (0, 5, 1), (0, 2, 1), (0, 6, 0), (0, 2, 0), (0, 6, 1), (1, 1, 0), (1, 3, 1)]
    + [(0, 1, 1), (0, 7, 0), (0, 1, 0), (0, 7, 1), (0, 0, 0), (0, 0, 1)]
)
LAST_FIRST = [(1, 0, 0), (1, 0, 1)]


def reduce_kernel(
    grads, momentum, out, own, other, zu, zd, yu, yd, shares, window,
    load_sem, other_send, other_recv, send_sem, recv_sem, share_sem,
):
    section = lax.axis_index("section")
    me = lax.axis_index("dp")
    z, y, c = place(me)
    boxes = (zu, zd, yu, yd)

    def device(nz, ny, nc):
        return (section, (nz * NY + ny) * 2 + nc)

    targets = (
        device(lax.rem(z + 1, NZ), y, c),
        device(lax.rem(z + NZ - 1, NZ), y, c),
        device(z, lax.rem(y + 1, NY), c),
        device(z, lax.rem(y + NY - 1, NY), c),
    )
    partner = device(z, y, 1 - c)

    def rows(q):
        return pl.ds(LOW[q], COUNT[q])

    def load(j, q):
        return pltpu.make_async_copy(
            grads.at[HALF * c + j, rows(q)], own.at[j, rows(q)], load_sem.at[j, q]
        )

    def cross(j, q):
        return pltpu.make_async_remote_copy(
            src_ref=grads.at[HALF * (1 - c) + j, rows(q)],
            dst_ref=other.at[j, rows(q)],
            send_sem=other_send.at[j, q],
            recv_sem=other_recv.at[j, q],
            device_id=partner,
            device_id_type=MESH,
        )

    def hop(j, q, way):
        return pltpu.make_async_remote_copy(
            src_ref=own.at[j, rows(q)],
            dst_ref=boxes[way].at[j, rows(q)],
            send_sem=send_sem.at[j, q],
            recv_sem=recv_sem.at[way, j, q],
            device_id=targets[way],
            device_id_type=MESH,
        )

    def total(j, q, terms):
        def body(i, carry):
            r = pl.ds(pl.multiple_of(LOW[q] + 16 * i, 16), 16)
            acc = own[j, r, :].astype(F32)
            for term in terms:
                acc = acc + term[j, r, :].astype(F32)
            own[j, r, :] = acc.astype(BF16)
            return carry

        lax.fori_loop(0, COUNT[q] // 16, body, 0)

    first = []
    for axis, d, half in FIRST + LAST_FIRST:
        for r in range(2 + axis):
            first.append((axis, d, half, r))

    def start(step, only):
        axis, d, half, r = step
        q = 2 * axis + half
        if only != "cross":
            j, valid = first_candidates(axis, d, z, y, c)[r]
            guarded(valid, lambda: load(j, q).start())
        if only != "load":
            k, fine = first_candidates(axis, d, z, y, 1 - c)[r]
            guarded(fine, lambda: cross(k, q).start())

    ahead = 20
    for step in first[:ahead]:
        start(step, "load")

    barrier = pltpu.get_barrier_semaphore()
    for target in targets + (partner,):
        pl.semaphore_signal(barrier, inc=1, device_id=target, device_id_type=MESH)
    shares[c, 0:MATRICES, :] = momentum[...].astype(F32)
    pl.semaphore_wait(barrier, 5)

    exchange = pltpu.make_async_remote_copy(
        src_ref=shares.at[c],
        dst_ref=shares.at[c],
        send_sem=share_sem.at[0],
        recv_sem=share_sem.at[1],
        device_id=partner,
        device_id_type=MESH,
    )
    exchange.start()
    for step in first[:ahead]:
        start(step, "cross")

    line = 9 * (me // 2)
    base = jnp.minimum(16 * (line // 16), HEIGHT - WINDOW)
    shift = line - base
    window[...] = jnp.zeros_like(window)
    exchange.wait()
    for core in range(2):

        @pl.when(c == core)
        def _():
            for source in range(2):
                for k in range(STRIPS):
                    at = STRIPS * source + k
                    window[at % 8, pl.ds(shift + at // 8, HALF, stride=WINDOW), :] = shares[
                        source, HALF * core : HALF * (core + 1), 128 * k : 128 * (k + 1)
                    ]

    scale = MOMENTUM_DECAY * MOMENTUM_DECAY / (1.0 + MOMENTUM_DECAY)

    def blend(j, q):
        for part in range(WINDOW // 16):
            top = base + 16 * part

            @pl.when(jnp.logical_and(top >= LOW[q], top < LOW[q] + COUNT[q]))
            def _():
                r = pl.ds(pl.multiple_of(top, 16), 16)
                from_window = pl.ds(pl.multiple_of(WINDOW * j + 16 * part, 16), 16)
                for block in range(8):
                    lanes = pl.ds(128 * block, 128)
                    own[j, r, lanes] = (
                        own[j, r, lanes].astype(F32) + scale * window[block, from_window, :]
                    ).astype(BF16)

    def first_step(step):
        axis, d, half, r = step
        q = 2 * axis + half
        j, valid = first_candidates(axis, d, z, y, c)[r]
        receives, sends = roles(axis, d, half)

        def body():
            load(j, q).wait()
            cross(j, q).wait_recv()
            for way in receives:
                hop(j, q, way).wait_recv()
            total(j, q, [other] + [boxes[way] for way in receives])
            blend(j, q)
            if sends is not None:
                hop(j, q, sends).start()

        guarded(valid, body)

    def second_step(axis, d, half):
        q = 2 * (1 - axis) + half
        if axis == 0:
            v = lax.rem(z + d + NZ - 3 * c, NZ)
            here = y
        else:
            v = lax.rem(z + NZ - 3 * c, NZ)
            here = lax.rem(y + d, NY)
        early = owner_y(v, c) == here
        late = jnp.logical_and(v < 3, owner_y(v + 8, c) == here)
        j = jnp.minimum(jnp.where(early, v, v + 8), HALF - 1)
        receives, sends = roles(axis, d, half)

        def body():
            for way in receives:
                hop(j, q, way).wait_recv()
            if receives:
                total(j, q, [boxes[way] for way in receives])
            if sends is not None:
                hop(j, q, sends).start()

        pl.when(jnp.logical_or(early, late))(body)

    for number, step in enumerate(first):
        if number + ahead < len(first):
            start(first[number + ahead], None)
        first_step(step)
        if step == (0, 0, 1, 1):
            second_step(1, 2, 0)
            second_step(1, 2, 1)
    for step in (
        [(0, 4, 0), (0, 4, 1), (0, 3, 1), (0, 5, 0), (1, 1, 1), (1, 3, 0), (1, 1, 0), (1, 3, 1)]
        + [(0, 3, 0), (0, 5, 1), (1, 0, 0), (1, 0, 1), (0, 2, 1), (0, 6, 0), (0, 2, 0), (0, 6, 1)]
        + [(0, 1, 1), (0, 7, 0), (0, 1, 0), (0, 7, 1), (0, 0, 0), (0, 0, 1)]
    ):
        second_step(*step)

    mine, is_owner = owned(me)

    @pl.when(is_owner)
    def _():
        out[...] = own[mine]

    @pl.when(jnp.logical_not(is_owner))
    def _():
        out[...] = jnp.zeros_like(out)

    def drain(j, carry):
        for q in range(4):
            cross(j, q).wait_send()

            @pl.when(jnp.logical_not(jnp.logical_and(is_owner, j == mine)))
            def _():
                hop(j, q, 0).wait_send()

        return carry

    lax.fori_loop(0, HALF, drain, 0)


def reduced(grads, momentum):
    matrix = (HALF, HEIGHT, BREADTH)
    return pl.pallas_call(
        reduce_kernel,
        out_shape=jax.ShapeDtypeStruct((HEIGHT, BREADTH), BF16),
        in_specs=[pl.BlockSpec(memory_space=pl.ANY), pl.BlockSpec(memory_space=pltpu.VMEM)],
        out_specs=pl.BlockSpec(memory_space=pltpu.VMEM),
        scratch_shapes=[pltpu.VMEM(matrix, BF16)] * 6
        + [
            pltpu.VMEM((2, 24, PORTION), F32),
            pltpu.VMEM((8, HALF * WINDOW, 128), F32),
            pltpu.SemaphoreType.DMA((HALF, 4)),
            pltpu.SemaphoreType.DMA((HALF, 4)),
            pltpu.SemaphoreType.DMA((HALF, 4)),
            pltpu.SemaphoreType.DMA((HALF, 4)),
            pltpu.SemaphoreType.DMA((4, HALF, 4)),
            pltpu.SemaphoreType.DMA((2,)),
        ],
        compiler_params=pltpu.CompilerParams(
            collective_id=0, has_side_effects=True, vmem_limit_bytes=56 << 20
        ),
        name="reduce_to_owners",
    )(grads, momentum)


def return_kernel(matrix, weights, out, flat, pieces, got, wide, send_sem, recv_sem):
    section = lax.axis_index("section")
    me = lax.axis_index("dp")
    mine, is_owner = owned(me)
    slot = HALF * lax.rem(me, 2) + mine

    barrier = pltpu.get_barrier_semaphore()

    def greet(j, carry):
        for core in range(2):
            owner = (owner_z(j, core) * NY + owner_y(j, core)) * 2 + core

            @pl.when(owner != me)
            def _():
                pl.semaphore_signal(
                    barrier, inc=1, device_id=(section, owner), device_id_type=MESH
                )

        return carry

    lax.fori_loop(0, HALF, greet, 0)

    def share(step):
        to = lax.rem(me + step, GROUPS)
        return pltpu.make_async_remote_copy(
            src_ref=pieces.at[to],
            dst_ref=got.at[slot],
            send_sem=send_sem,
            recv_sem=recv_sem,
            device_id=(section, to),
            device_id_type=MESH,
        )

    @pl.when(is_owner)
    def _():
        for k in range(8):
            flat[pl.ds(k, HEIGHT, stride=8), :] = matrix[:, 128 * k : 128 * (k + 1)].astype(F32)

        def cut(pair, carry):
            both = flat[pl.ds(pl.multiple_of(2 * STRIPS * pair, 8), 2 * STRIPS), :]
            pad = jnp.zeros((STRIP_ROWS - STRIPS, 128), F32)
            pieces[2 * pair] = jnp.concatenate([both[:STRIPS], pad]).astype(BF16)
            pieces[2 * pair + 1] = jnp.concatenate([both[STRIPS:], pad]).astype(BF16)
            return carry

        lax.fori_loop(0, GROUPS // 2, cut, 0)
        pl.semaphore_wait(barrier, GROUPS - 1)

        def send(step, carry):
            share(step).start()
            return carry

        lax.fori_loop(1, GROUPS, send, 0)
        got[slot] = pieces[me]

    def arrived(number):
        return pltpu.make_async_remote_copy(
            src_ref=pieces.at[pl.ds(0, number)],
            dst_ref=got.at[pl.ds(0, number)],
            send_sem=send_sem,
            recv_sem=recv_sem,
            device_id=(section, me),
            device_id_type=MESH,
        )

    @pl.when(is_owner)
    def _():
        arrived(MATRICES - 1).wait_recv()

    @pl.when(jnp.logical_not(is_owner))
    def _():
        arrived(MATRICES).wait_recv()

    for m in range(MATRICES):
        wide[STRIP_ROWS * m : STRIP_ROWS * (m + 1), :] = got[m].astype(F32)
    factor = 0.2 * math.sqrt(max(HEIGHT, BREADTH))
    for k in range(STRIPS):
        lanes = slice(128 * k, 128 * (k + 1))
        update = wide[pl.ds(k, MATRICES, stride=STRIP_ROWS), :]
        out[:, lanes] = (
            weights[:, lanes].astype(F32) * (1.0 - LEARN_RATE * DECAY_RATE)
            - LEARN_RATE * factor * update
        ).astype(BF16)

    @pl.when(is_owner)
    def _():
        pltpu.make_async_copy(
            pieces.at[pl.ds(0, GROUPS - 1)], pieces.at[pl.ds(0, GROUPS - 1)], send_sem
        ).wait()


def returned(matrix, weights):
    return pl.pallas_call(
        return_kernel,
        out_shape=jax.ShapeDtypeStruct((MATRICES, PORTION), BF16),
        in_specs=[pl.BlockSpec(memory_space=pltpu.VMEM)] * 2,
        out_specs=pl.BlockSpec(memory_space=pltpu.VMEM),
        scratch_shapes=[
            pltpu.VMEM((GROUPS * STRIPS, 128), F32),
            pltpu.VMEM((GROUPS, STRIP_ROWS, 128), BF16),
            pltpu.VMEM((MATRICES, STRIP_ROWS, 128), BF16),
            pltpu.VMEM((MATRICES * STRIP_ROWS, 128), F32),
            pltpu.SemaphoreType.DMA,
            pltpu.SemaphoreType.DMA,
        ],
        compiler_params=pltpu.CompilerParams(
            collective_id=1, has_side_effects=True, vmem_limit_bytes=32 << 20
        ),
        name="return_shares",
    )(matrix, weights)


def newton(current):
    for _ in range(ITERS):
        gram = jnp.einsum("ij,lj->il", current, current, preferred_element_type=F32).astype(BF16)
        square = jnp.dot(gram, gram, preferred_element_type=F32)
        polynomial = (QUINTIC_B * gram.astype(F32) + QUINTIC_C * square).astype(BF16)
        mixed = jnp.dot(polynomial, current, preferred_element_type=F32)
        current = (QUINTIC_A * current.astype(F32) + mixed).astype(BF16)
    return current


def local(grads, momentum, weights):
    summed = reduced(grads[0, 0], momentum[0])
    blended = (1.0 + MOMENTUM_DECAY) * summed.astype(F32)
    frobenius = jnp.sqrt(jnp.sum(blended * blended)) + EPSILON
    orthogonal = newton((blended / frobenius).astype(BF16))
    return returned(orthogonal, weights[0])[None]


def solution(mesh):
    placed = (
        P("section", "dp", None, None, None),
        P("section", None, "dp"),
        P("section", None, "dp"),
    )
    return jax.shard_map(
        local, mesh=mesh, in_specs=placed, out_specs=P("section", None, "dp"), check_vma=False
    )
```

```python
import math

import jax
import jax.numpy as jnp
from jax import lax
from jax.experimental import pallas as pl
from jax.experimental.pallas import tpu as pltpu
from jax.sharding import PartitionSpec as P

ITERS = 5
QUINTIC_A = 3.4445
QUINTIC_B = -4.775
QUINTIC_C = 2.0315
MOMENTUM_DECAY = 0.95
LEARN_RATE = 0.5
DECAY_RATE = 0.1
EPSILON = 1e-07

NZ, NY = 8, 4
MATRICES, HEIGHT, BREADTH = 22, 288, 1024
HALF = MATRICES // 2
GROUPS = 64
PORTION = HEIGHT * BREADTH // GROUPS
STRIPS = PORTION // 128
STRIP_ROWS = 48
WINDOW = 32
ROUNDS = 6
ROWS = HEIGHT // ROUNDS
LOW = (0, 384)
WIDTH = (384, 640)
MESH = pl.DeviceIdType.MESH
F32, BF16 = jnp.float32, jnp.bfloat16


def place(dp):
    return dp // 8, lax.rem(dp // 2, NY), lax.rem(dp, 2)


def owner_z(j, c):
    return lax.rem(j + 4 * c, NZ)


def owner_y(j, c):
    return lax.rem(j + j // 8 + 2 * c, NY)


def owned_at(z, y, c):
    v = lax.rem(z + NZ - 4 * c, NZ)
    first = owner_y(v, c) == y
    second = jnp.logical_and(v < 3, owner_y(v + 8, c) == y)
    return jnp.minimum(jnp.where(first, v, v + 8), HALF - 1), jnp.logical_or(first, second)


def candidates(axis, d, z, y, c):
    if axis == 0:
        u = lax.rem(z + d + NZ - 4 * c, NZ)
        return [(u, None), (jnp.minimum(u + 8, HALF - 1), u < 3)]
    u = lax.rem(y + d + NY - 2 * c, NY)
    return [(u, None), (u + 4, None), (jnp.minimum(u + 7, HALF - 1), u >= 1)]


def guarded(valid, body):
    if valid is None:
        body()
    else:
        pl.when(valid)(body)


def roles(axis, d):
    n = NZ if axis == 0 else NY
    far = n // 2
    up, down = 2 * axis, 2 * axis + 1
    receives, sends = [], []
    if d < far - 1:
        receives.append((up, None))
    if d == far - 1:
        receives.append((up, 0))
    if d == 0 or d > far + 1:
        receives.append((down, None))
    if d == far + 1:
        receives.append((down, 1))
    if 1 <= d < far:
        sends.append((up, None))
    if d == far:
        sends += [(up, 0), (down, 1)]
    if d > far:
        sends.append((down, None))
    return receives, sends


ORDER = (
    (1, 0, 4, 0), (1, 1, 2, 0),
    (1, 0, 3, 1), (1, 0, 5, 1), (1, 1, 1, 1), (1, 1, 3, 1),
    (1, 0, 2, 2), (1, 0, 6, 2), (1, 1, 0, 2), (2, 0, 4, 2),
    (1, 0, 1, 3), (1, 0, 7, 3), (2, 0, 3, 3), (2, 0, 5, 3),
    (1, 0, 0, 4), (2, 1, 2, 4), (2, 0, 2, 4), (2, 0, 6, 4),
    (2, 1, 1, 5), (2, 1, 3, 5), (2, 0, 1, 5), (2, 0, 7, 5),
    (2, 1, 0, 6), (2, 0, 0, 6),
)
LAG = 6


def kernel(
    grads, momentum, weights, out, own, other, box, shares, window, current, flat, pieces, got, wide,
    load_sem, cross_send, cross_recv, send_sem, recv_sem, share_sem, piece_send, piece_recv,
):
    section = lax.axis_index("section")
    me = lax.axis_index("dp")
    z, y, c = place(me)
    mine, is_owner = owned_at(z, y, c)
    is_guest = jnp.logical_not(is_owner)

    def device(nz, ny, nc):
        return (section, (nz * NY + ny) * 2 + nc)

    targets = (
        device(lax.rem(z + 1, NZ), y, c),
        device(lax.rem(z + NZ - 1, NZ), y, c),
        device(z, lax.rem(y + 1, NY), c),
        device(z, lax.rem(y + NY - 1, NY), c),
    )
    partner = device(z, y, 1 - c)

    def rows(k):
        return pl.ds(pl.multiple_of(ROWS * k, 16), ROWS)

    def load(k):
        return pltpu.make_async_copy(
            grads.at[pl.ds(HALF * c, HALF), rows(k)], own.at[:, rows(k)], load_sem.at[k]
        )

    def cross(k):
        return pltpu.make_async_remote_copy(
            src_ref=grads.at[pl.ds(HALF * (1 - c), HALF), rows(k)],
            dst_ref=other.at[:, rows(k)],
            send_sem=cross_send.at[k],
            recv_sem=cross_recv.at[k],
            device_id=partner,
            device_id_type=MESH,
        )

    def hop(j, k, t, way):
        part = (rows(k), pl.ds(LOW[t], WIDTH[t]))
        return pltpu.make_async_remote_copy(
            src_ref=own.at[j, part[0], part[1]],
            dst_ref=box.at[way, j, part[0], part[1]],
            send_sem=send_sem,
            recv_sem=recv_sem.at[way, k, j, t],
            device_id=targets[way],
            device_id_type=MESH,
        )

    for k in range(ROUNDS):
        load(k).start()

    barrier = pltpu.get_barrier_semaphore()
    for target in targets + (partner,):
        pl.semaphore_signal(barrier, inc=1, device_id=target, device_id_type=MESH)

    shares[c, 0:MATRICES, :] = momentum[...].astype(F32)

    pl.semaphore_wait(barrier, 5)

    exchange = pltpu.make_async_remote_copy(
        src_ref=shares.at[c],
        dst_ref=shares.at[c],
        send_sem=share_sem.at[0],
        recv_sem=share_sem.at[1],
        device_id=partner,
        device_id_type=MESH,
    )
    exchange.start()
    for k in range(ROUNDS):
        cross(k).start()

    line = 9 * (me // 2)
    base = jnp.minimum(16 * (line // 16), HEIGHT - WINDOW)
    shift = line - base
    window[...] = jnp.zeros_like(window)
    exchange.wait()
    for core in range(2):

        @pl.when(c == core)
        def _():
            for source in range(2):
                for k in range(STRIPS):
                    at = STRIPS * source + k
                    window[at % 8, pl.ds(shift + at // 8, HALF, stride=WINDOW), :] = shares[
                        source, HALF * core : HALF * (core + 1), 128 * k : 128 * (k + 1)
                    ]

    scale = MOMENTUM_DECAY * MOMENTUM_DECAY / (1.0 + MOMENTUM_DECAY)

    def combine(k):
        load(k).wait()
        cross(k).wait_recv()

        def add(j, carry):
            own[j, rows(k), :] = (
                own[j, rows(k), :].astype(F32) + other[j, rows(k), :].astype(F32)
            ).astype(BF16)
            return carry

        lax.fori_loop(0, HALF, add, 0)
        for part in range(WINDOW // 16):
            top = base + 16 * part

            @pl.when(top // ROWS == k)
            def _():
                r = pl.ds(pl.multiple_of(top, 16), 16)

                def blend(j, carry):
                    from_window = pl.ds(pl.multiple_of(WINDOW * j + 16 * part, 16), 16)
                    for block in range(8):
                        lanes = pl.ds(128 * block, 128)
                        own[j, r, lanes] = (
                            own[j, r, lanes].astype(F32) + scale * window[block, from_window, :]
                        ).astype(BF16)
                    return carry

                lax.fori_loop(0, HALF, blend, 0)

    steps = []
    for phase, axis, d, lag in ORDER:
        if phase == 1:
            found = candidates(axis, d, z, y, c)
        elif axis == 0:
            found = [owned_at(lax.rem(z + d, NZ), y, c)]
        else:
            found = [owned_at(z, lax.rem(y + d, NY), c)]
        for j, valid in found:
            steps.append((axis if phase == 1 else 1 - axis, j, valid, lag, *roles(axis, d)))

    def step(k, parity, t, j, receives, sends):
        part = (rows(k), pl.ds(LOW[t], WIDTH[t]))

        def take(ways):
            for way in ways:
                hop(j, k, t, way).wait_recv()
            total = own[j, part[0], part[1]].astype(F32)
            for way in ways:
                total = total + box[way, j, part[0], part[1]].astype(F32)
            own[j, part[0], part[1]] = total.astype(BF16)

        always = [way for way, when in receives if when is None]
        if always:
            take(always)
        for way, when in receives:
            if when is not None:
                pl.when(parity == when)(lambda way=way: take([way]))
        for way, when in sends:
            guarded(None if when is None else parity == when, lambda way=way: hop(j, k, t, way).start())

    combine(0)

    def body(i, carry):
        for t, j, valid, lag, receives, sends in steps:
            k = i - lag
            live = jnp.logical_and(k >= 0, k < ROUNDS)
            if valid is not None:
                live = jnp.logical_and(live, valid)
            pl.when(live)(
                lambda k=k, t=t, j=j, receives=receives, sends=sends: step(
                    k, lax.rem(k + c, 2), t, j, receives, sends
                )
            )

        @pl.when(i + 1 < ROUNDS)
        def _():
            combine(i + 1)

        return carry

    lax.fori_loop(0, ROUNDS + LAG, body, 0)

    slot = HALF * c + mine

    def share(distance):
        to = lax.rem(me + distance, GROUPS)
        return pltpu.make_async_remote_copy(
            src_ref=pieces.at[to],
            dst_ref=got.at[slot],
            send_sem=piece_send,
            recv_sem=piece_recv,
            device_id=(section, to),
            device_id_type=MESH,
        )

    @pl.when(is_owner)
    def _():
        blended = (1.0 + MOMENTUM_DECAY) * own[mine].astype(F32)
        norm = jnp.sqrt(jnp.sum(blended * blended, keepdims=True)) + EPSILON
        current[...] = (blended / norm).astype(BF16)

        def newton(_, carry):
            x = current[...]
            gram = lax.dot_general(
                x, x, (((1,), (1,)), ((), ())), preferred_element_type=F32
            ).astype(BF16)
            square = jnp.dot(gram, gram, preferred_element_type=F32)
            polynomial = (QUINTIC_B * gram.astype(F32) + QUINTIC_C * square).astype(BF16)
            mixed = jnp.dot(polynomial, x, preferred_element_type=F32)
            current[...] = (QUINTIC_A * x.astype(F32) + mixed).astype(BF16)
            return carry

        lax.fori_loop(0, ITERS, newton, 0)
        for k in range(8):
            flat[pl.ds(k, HEIGHT, stride=8), :] = current[:, 128 * k : 128 * (k + 1)].astype(F32)

        def cut(pair, carry):
            both = flat[pl.ds(pl.multiple_of(2 * STRIPS * pair, 8), 2 * STRIPS), :]
            pad = jnp.zeros((STRIP_ROWS - STRIPS, 128), F32)
            pieces[2 * pair] = jnp.concatenate([both[:STRIPS], pad]).astype(BF16)
            pieces[2 * pair + 1] = jnp.concatenate([both[STRIPS:], pad]).astype(BF16)
            return carry

        lax.fori_loop(0, GROUPS // 2, cut, 0)

        def send(distance, carry):
            share(distance).start()
            return carry

        lax.fori_loop(1, GROUPS, send, 0)
        got[slot] = pieces[me]

    for k in range(ROUNDS):
        cross(k).wait_send()

    def sent(number):
        pltpu.make_async_copy(own.at[pl.ds(0, number)], own.at[pl.ds(0, number)], send_sem).wait()

    def arrived(number):
        pltpu.make_async_copy(
            got.at[pl.ds(0, number)], got.at[pl.ds(0, number)], piece_recv
        ).wait()

    @pl.when(is_owner)
    def _():
        sent(HALF - 1)
        arrived(MATRICES - 1)

    @pl.when(is_guest)
    def _():
        sent(HALF)
        arrived(MATRICES)

    for m in range(MATRICES):
        wide[STRIP_ROWS * m : STRIP_ROWS * (m + 1), :] = got[m].astype(F32)
    factor = 0.2 * math.sqrt(max(HEIGHT, BREADTH))
    for k in range(STRIPS):
        lanes = slice(128 * k, 128 * (k + 1))
        update = wide[pl.ds(k, MATRICES, stride=STRIP_ROWS), :]
        out[:, lanes] = (
            weights[:, lanes].astype(F32) * (1.0 - LEARN_RATE * DECAY_RATE)
            - LEARN_RATE * factor * update
        ).astype(BF16)

    @pl.when(is_owner)
    def _():
        pltpu.make_async_copy(
            pieces.at[pl.ds(0, GROUPS - 1)], pieces.at[pl.ds(0, GROUPS - 1)], piece_send
        ).wait()


def local(grads, momentum, weights):
    matrix = (HALF, HEIGHT, BREADTH)
    dma = pltpu.SemaphoreType.DMA
    return pl.pallas_call(
        kernel,
        out_shape=jax.ShapeDtypeStruct((MATRICES, PORTION), BF16),
        in_specs=[pl.BlockSpec(memory_space=pl.ANY)] + [pl.BlockSpec(memory_space=pltpu.VMEM)] * 2,
        out_specs=pl.BlockSpec(memory_space=pltpu.VMEM),
        scratch_shapes=[
            pltpu.VMEM(matrix, BF16),
            pltpu.VMEM(matrix, BF16),
            pltpu.VMEM((4, *matrix), BF16),
            pltpu.VMEM((2, 24, PORTION), F32),
            pltpu.VMEM((8, HALF * WINDOW, 128), F32),
            pltpu.VMEM((HEIGHT, BREADTH), BF16),
            pltpu.VMEM((GROUPS * STRIPS, 128), F32),
            pltpu.VMEM((GROUPS, STRIP_ROWS, 128), BF16),
            pltpu.VMEM((MATRICES, STRIP_ROWS, 128), BF16),
            pltpu.VMEM((MATRICES * STRIP_ROWS, 128), F32),
            dma((ROUNDS,)),
            dma((ROUNDS,)),
            dma((ROUNDS,)),
            dma,
            dma((4, ROUNDS, HALF, 2)),
            dma((2,)),
            dma,
            dma,
        ],
        compiler_params=pltpu.CompilerParams(
            collective_id=0, has_side_effects=True, vmem_limit_bytes=56 << 20
        ),
        name="muon_step",
    )(grads[0, 0], momentum[0], weights[0])[None]


def solution(mesh):
    placed = (
        P("section", "dp", None, None, None),
        P("section", None, "dp"),
        P("section", None, "dp"),
    )
    return jax.shard_map(
        local, mesh=mesh, in_specs=placed, out_specs=P("section", None, "dp"), check_vma=False
    )
```

```python
import math

import jax
import jax.numpy as jnp
from jax import lax
from jax.experimental import pallas as pl
from jax.experimental.pallas import tpu as pltpu
from jax.sharding import PartitionSpec as P

ITERS = 5
QUINTIC_A = 3.4445
QUINTIC_B = -4.775
QUINTIC_C = 2.0315
MOMENTUM_DECAY = 0.95
LEARN_RATE = 0.5
DECAY_RATE = 0.1
EPSILON = 1e-07

NZ, NY = 8, 4
MATRICES, HEIGHT, BREADTH = 22, 288, 1024
HALF = MATRICES // 2
GROUPS = 64
PORTION = HEIGHT * BREADTH // GROUPS
STRIPS = PORTION // 128
STRIP_ROWS = 48
WINDOW = 32
QUARTER = HEIGHT // 4
ROUNDS = 6
ROWS = HEIGHT // ROUNDS
LOW = (0, 384)
WIDTH = (384, 640)
MESH = pl.DeviceIdType.MESH
F32, BF16 = jnp.float32, jnp.bfloat16


def place(dp):
    return dp // 8, lax.rem(dp // 2, NY), lax.rem(dp, 2)


def owner_z(j, c):
    return lax.rem(j + 4 * c, NZ)


def owner_y(j, c):
    return lax.rem(j + j // 8 + 2 * c, NY)


def owned_at(z, y, c):
    v = lax.rem(z + NZ - 4 * c, NZ)
    first = owner_y(v, c) == y
    second = jnp.logical_and(v < 3, owner_y(v + 8, c) == y)
    return jnp.minimum(jnp.where(first, v, v + 8), HALF - 1), jnp.logical_or(first, second)


def candidates(axis, d, z, y, c):
    if axis == 0:
        u = lax.rem(z + d + NZ - 4 * c, NZ)
        return [(u, None), (jnp.minimum(u + 8, HALF - 1), u < 3)]
    u = lax.rem(y + d + NY - 2 * c, NY)
    return [(u, None), (u + 4, None), (jnp.minimum(u + 7, HALF - 1), u >= 1)]


def guarded(valid, body):
    if valid is None:
        body()
    else:
        pl.when(valid)(body)


Z_UP, Z_DOWN, Y_UP, Y_DOWN, Z_UP_TWO, Z_DOWN_TWO, Y_UP_TWO = range(7)
FAR = 4


def roles(phase, axis, d):
    n = NZ if axis == 0 else NY
    far = n // 2
    up, down = 2 * axis, 2 * axis + 1
    if phase == 2 and axis == 1:
        if d == 0:
            return [(up, None), (down, None), (FAR, None)], []
        if d == far:
            return [], [(Y_UP_TWO, FAR, None)]
        return [], [(up, up, None) if d < far else (down, down, None)]
    receives, sends = [], []
    if d < far - 1:
        receives.append((up, None))
    if d == 0 or d > far + 1:
        receives.append((down, None))
    if phase == 1:
        if d == far - 1:
            receives.append((up, 0))
        if d == far + 1:
            receives.append((down, 1))
    else:
        if d == far - 2:
            receives.append((down, 0))
        if d == far + 2:
            receives.append((up, 1))
    if 1 <= d < far:
        sends.append((up, up, None))
    if d == far and phase == 1:
        sends += [(up, up, 0), (down, down, 1)]
    if d == far and phase == 2:
        sends += [(Z_UP_TWO, down, 0), (Z_DOWN_TWO, up, 1)]
    if d > far:
        sends.append((down, down, None))
    return receives, sends


ORDER = (
    (1, 0, 4, 0), (1, 1, 2, 0),
    (1, 0, 3, 1), (1, 0, 5, 1), (1, 1, 1, 1), (1, 1, 3, 1),
    (1, 0, 2, 2), (1, 0, 6, 2), (1, 1, 0, 2), (2, 0, 4, 2), (2, 0, 3, 2), (2, 0, 5, 2),
    (1, 0, 1, 3), (1, 0, 7, 3), (2, 0, 2, 3), (2, 0, 6, 3),
    (1, 0, 0, 4), (2, 1, 2, 4), (2, 1, 1, 4), (2, 1, 3, 4), (2, 0, 1, 4), (2, 0, 7, 4),
    (2, 1, 0, 5), (2, 0, 0, 5),
)
LAG = 5


def kernel(
    grads, momentum, weights, out, own, other, box, shares, window, near, current, last, scaled, flat, pieces, got, wide,
    load_sem, cross_send, cross_recv, send_sem, recv_sem, share_sem, near_sem, piece_send, piece_recv,
):
    section = lax.axis_index("section")
    me = lax.axis_index("dp")
    z, y, c = place(me)
    mine, is_owner = owned_at(z, y, c)
    is_guest = jnp.logical_not(is_owner)

    def device(nz, ny, nc):
        return (section, (nz * NY + ny) * 2 + nc)

    targets = (
        device(lax.rem(z + 1, NZ), y, c),
        device(lax.rem(z + NZ - 1, NZ), y, c),
        device(z, lax.rem(y + 1, NY), c),
        device(z, lax.rem(y + NY - 1, NY), c),
        device(lax.rem(z + 2, NZ), y, c),
        device(lax.rem(z + NZ - 2, NZ), y, c),
        device(z, lax.rem(y + 2, NY), c),
    )
    partner = device(z, y, 1 - c)

    def rows(k):
        return pl.ds(pl.multiple_of(ROWS * k, 16), ROWS)

    def load(k):
        return pltpu.make_async_copy(
            grads.at[pl.ds(HALF * c, HALF), rows(k)], own.at[:, rows(k)], load_sem.at[k]
        )

    def cross(k):
        return pltpu.make_async_remote_copy(
            src_ref=grads.at[pl.ds(HALF * (1 - c), HALF), rows(k)],
            dst_ref=other.at[:, rows(k)],
            send_sem=cross_send.at[k],
            recv_sem=cross_recv.at[k],
            device_id=partner,
            device_id_type=MESH,
        )

    def hop(j, k, t, target, way):
        part = (rows(k), pl.ds(LOW[t], WIDTH[t]))
        return pltpu.make_async_remote_copy(
            src_ref=own.at[j, part[0], part[1]],
            dst_ref=near.at[part[0], :] if way == FAR else box.at[way, j, part[0], part[1]],
            send_sem=send_sem,
            recv_sem=near_sem.at[k] if way == FAR else recv_sem.at[way, k, j, t],
            device_id=targets[target],
            device_id_type=MESH,
        )

    for k in range(ROUNDS):
        load(k).start()

    barrier = pltpu.get_barrier_semaphore()
    for target in targets[:4] + (partner,):
        pl.semaphore_signal(barrier, inc=1, device_id=target, device_id_type=MESH)

    shares[c, 0:MATRICES, :] = momentum[...].astype(F32)

    pl.semaphore_wait(barrier, 5)

    exchange = pltpu.make_async_remote_copy(
        src_ref=shares.at[c],
        dst_ref=shares.at[c],
        send_sem=share_sem.at[0],
        recv_sem=share_sem.at[1],
        device_id=partner,
        device_id_type=MESH,
    )
    exchange.start()
    for k in range(ROUNDS):
        cross(k).start()

    line = 9 * (me // 2)
    base = jnp.minimum(16 * (line // 16), HEIGHT - WINDOW)
    shift = line - base
    window[...] = jnp.zeros_like(window)
    exchange.wait()
    for core in range(2):

        @pl.when(c == core)
        def _():
            for source in range(2):
                for k in range(STRIPS):
                    at = STRIPS * source + k
                    window[at % 8, pl.ds(shift + at // 8, HALF, stride=WINDOW), :] = shares[
                        source, HALF * core : HALF * (core + 1), 128 * k : 128 * (k + 1)
                    ]

    scale = MOMENTUM_DECAY * MOMENTUM_DECAY / (1.0 + MOMENTUM_DECAY)

    def combine(k):
        load(k).wait()
        cross(k).wait_recv()

        def add(j, carry):
            own[j, rows(k), :] = (
                own[j, rows(k), :].astype(F32) + other[j, rows(k), :].astype(F32)
            ).astype(BF16)
            return carry

        lax.fori_loop(0, HALF, add, 0)
        for part in range(WINDOW // 16):
            top = base + 16 * part

            @pl.when(top // ROWS == k)
            def _():
                r = pl.ds(pl.multiple_of(top, 16), 16)

                def blend(j, carry):
                    from_window = pl.ds(pl.multiple_of(WINDOW * j + 16 * part, 16), 16)
                    for block in range(8):
                        lanes = pl.ds(128 * block, 128)
                        own[j, r, lanes] = (
                            own[j, r, lanes].astype(F32) + scale * window[block, from_window, :]
                        ).astype(BF16)
                    return carry

                lax.fori_loop(0, HALF, blend, 0)

    steps = []
    for phase, axis, d, lag in ORDER:
        if phase == 1:
            found = candidates(axis, d, z, y, c)
        elif axis == 0:
            found = [owned_at(lax.rem(z + d, NZ), y, c)]
        else:
            found = [owned_at(z, lax.rem(y + d, NY), c)]
        for j, valid in found:
            steps.append((axis if phase == 1 else 1 - axis, j, valid, lag, *roles(phase, axis, d)))

    def step(k, parity, t, j, receives, sends):
        part = (rows(k), pl.ds(LOW[t], WIDTH[t]))

        def take(ways):
            for way in ways:
                hop(j, k, t, 0, way).wait_recv()
            total = own[j, part[0], part[1]].astype(F32)
            for way in ways:
                if way == FAR:
                    total = total + near[part[0], :].astype(F32)
                else:
                    total = total + box[way, j, part[0], part[1]].astype(F32)
            own[j, part[0], part[1]] = total.astype(BF16)

        always = [way for way, when in receives if when is None]
        if always:
            take(always)
        for way, when in receives:
            if when is not None:
                pl.when(parity == when)(lambda way=way: take([way]))
        for target, way, when in sends:
            guarded(
                None if when is None else parity == when,
                lambda target=target, way=way: hop(j, k, t, target, way).start(),
            )

    combine(0)

    def body(i, carry):
        for t, j, valid, lag, receives, sends in steps:
            k = i - lag
            live = jnp.logical_and(k >= 0, k < ROUNDS)
            if valid is not None:
                live = jnp.logical_and(live, valid)
            pl.when(live)(
                lambda k=k, t=t, j=j, receives=receives, sends=sends: step(
                    k, lax.rem(k + c, 2), t, j, receives, sends
                )
            )

        @pl.when(i + 1 < ROUNDS)
        def _():
            combine(i + 1)

        return carry

    lax.fori_loop(0, ROUNDS + LAG, body, 0)

    slot = HALF * c + mine

    def share(to):
        return pltpu.make_async_remote_copy(
            src_ref=pieces.at[to],
            dst_ref=got.at[slot],
            send_sem=piece_send,
            recv_sem=piece_recv,
            device_id=(section, to),
            device_id_type=MESH,
        )

    @pl.when(is_owner)
    def _():
        blended = (1.0 + MOMENTUM_DECAY) * own[mine].astype(F32)
        norm = jnp.sqrt(jnp.sum(blended * blended, keepdims=True)) + EPSILON
        current[...] = (blended / norm).astype(BF16)

        def newton(_, carry):
            x = current[...]
            gram = lax.dot_general(
                x, x, (((1,), (1,)), ((), ())), preferred_element_type=F32
            ).astype(BF16)
            square = jnp.dot(gram, gram, preferred_element_type=F32)
            polynomial = (QUINTIC_B * gram.astype(F32) + QUINTIC_C * square).astype(BF16)
            mixed = jnp.dot(polynomial, x, preferred_element_type=F32)
            current[...] = (QUINTIC_A * x.astype(F32) + mixed).astype(BF16)
            return carry

        lax.fori_loop(0, ITERS - 1, newton, 0)
        x = current[...]
        gram = lax.dot_general(
            x, x, (((1,), (1,)), ((), ())), preferred_element_type=F32
        ).astype(BF16)
        square = jnp.dot(gram, gram, preferred_element_type=F32)
        last[...] = QUINTIC_B * gram.astype(F32) + QUINTIC_C * square
        scaled[...] = QUINTIC_A * x.astype(F32)

        def quarter(i, carry):
            ahead = jnp.where(i == 0, 2, jnp.where(i == 1, 1, jnp.where(i == 2, 3, 0)))
            q = lax.rem(z // 2 + ahead, 4)
            r = pl.ds(pl.multiple_of(QUARTER * q, 8), QUARTER)
            mixed = jnp.dot(last[r, :].astype(BF16), current[...], preferred_element_type=F32)
            new = scaled[r, :] + mixed
            for k in range(8):
                flat[pl.ds(k, QUARTER, stride=8), :] = new[:, 128 * k : 128 * (k + 1)]
            pad = jnp.zeros((STRIP_ROWS - STRIPS, 128), F32)
            for pair in range(8):
                both = flat[2 * STRIPS * pair : 2 * STRIPS * (pair + 1), :]
                to = 16 * q + 2 * pair
                pieces[to] = jnp.concatenate([both[:STRIPS], pad]).astype(BF16)
                pieces[to + 1] = jnp.concatenate([both[STRIPS:], pad]).astype(BF16)

            def send(e, carry):
                to = 16 * q + e

                @pl.when(to != me)
                def _():
                    share(to).start()

                return carry

            lax.fori_loop(0, 16, send, 0)
            return carry

        lax.fori_loop(0, 4, quarter, 0)
        got[slot] = pieces[me]

    for k in range(ROUNDS):
        cross(k).wait_send()

    def sent(number):
        pltpu.make_async_copy(own.at[pl.ds(0, number)], own.at[pl.ds(0, number)], send_sem).wait()

    def arrived(number):
        pltpu.make_async_copy(
            got.at[pl.ds(0, number)], got.at[pl.ds(0, number)], piece_recv
        ).wait()

    @pl.when(is_owner)
    def _():
        sent(HALF - 1)
        arrived(MATRICES - 1)

    @pl.when(is_guest)
    def _():
        sent(HALF)
        arrived(MATRICES)

    for m in range(MATRICES):
        wide[STRIP_ROWS * m : STRIP_ROWS * (m + 1), :] = got[m].astype(F32)
    factor = 0.2 * math.sqrt(max(HEIGHT, BREADTH))
    for k in range(STRIPS):
        lanes = slice(128 * k, 128 * (k + 1))
        update = wide[pl.ds(k, MATRICES, stride=STRIP_ROWS), :]
        out[:, lanes] = (
            weights[:, lanes].astype(F32) * (1.0 - LEARN_RATE * DECAY_RATE)
            - LEARN_RATE * factor * update
        ).astype(BF16)

    @pl.when(is_owner)
    def _():
        pltpu.make_async_copy(
            pieces.at[pl.ds(0, GROUPS - 1)], pieces.at[pl.ds(0, GROUPS - 1)], piece_send
        ).wait()


def local(grads, momentum, weights):
    matrix = (HALF, HEIGHT, BREADTH)
    dma = pltpu.SemaphoreType.DMA
    return pl.pallas_call(
        kernel,
        out_shape=jax.ShapeDtypeStruct((MATRICES, PORTION), BF16),
        in_specs=[pl.BlockSpec(memory_space=pl.ANY)] + [pl.BlockSpec(memory_space=pltpu.VMEM)] * 2,
        out_specs=pl.BlockSpec(memory_space=pltpu.VMEM),
        scratch_shapes=[
            pltpu.VMEM(matrix, BF16),
            pltpu.VMEM(matrix, BF16),
            pltpu.VMEM((4, *matrix), BF16),
            pltpu.VMEM((2, 24, PORTION), F32),
            pltpu.VMEM((8, HALF * WINDOW, 128), F32),
            pltpu.VMEM((HEIGHT, WIDTH[0]), BF16),
            pltpu.VMEM((HEIGHT, BREADTH), BF16),
            pltpu.VMEM((HEIGHT, HEIGHT), F32),
            pltpu.VMEM((HEIGHT, BREADTH), F32),
            pltpu.VMEM((QUARTER * 8, 128), F32),
            pltpu.VMEM((GROUPS, STRIP_ROWS, 128), BF16),
            pltpu.VMEM((MATRICES, STRIP_ROWS, 128), BF16),
            pltpu.VMEM((MATRICES * STRIP_ROWS, 128), F32),
            dma((ROUNDS,)),
            dma((ROUNDS,)),
            dma((ROUNDS,)),
            dma,
            dma((4, ROUNDS, HALF, 2)),
            dma((2,)),
            dma((ROUNDS,)),
            dma,
            dma,
        ],
        compiler_params=pltpu.CompilerParams(
            collective_id=0, has_side_effects=True, vmem_limit_bytes=56 << 20
        ),
        name="muon_step",
    )(grads[0, 0], momentum[0], weights[0])[None]


def solution(mesh):
    placed = (
        P("section", "dp", None, None, None),
        P("section", None, "dp"),
        P("section", None, "dp"),
    )
    return jax.shard_map(
        local, mesh=mesh, in_specs=placed, out_specs=P("section", None, "dp"), check_vma=False
    )
```

```python
import math

import jax
import jax.numpy as jnp
from jax import lax
from jax.experimental import pallas as pl
from jax.experimental.pallas import tpu as pltpu
from jax.sharding import PartitionSpec as P

ITERS = 5
QUINTIC_A = 3.4445
QUINTIC_B = -4.775
QUINTIC_C = 2.0315
MOMENTUM_DECAY = 0.95
LEARN_RATE = 0.5
DECAY_RATE = 0.1
EPSILON = 1e-07

NZ, NY = 8, 4
MATRICES, HEIGHT, BREADTH = 22, 288, 1024
HALF = MATRICES // 2
GROUPS = 64
PORTION = HEIGHT * BREADTH // GROUPS
STRIPS = PORTION // 128
STRIP_ROWS = 48
WINDOW = 32
QUARTER = HEIGHT // 4
ROUNDS = 6
ROWS = HEIGHT // ROUNDS
LOW = (0, 384)
WIDTH = (384, 640)
MESH = pl.DeviceIdType.MESH
F32, BF16 = jnp.float32, jnp.bfloat16


def place(dp):
    return dp // 8, lax.rem(dp // 2, NY), lax.rem(dp, 2)


def owner_z(j, c):
    return lax.rem(j + 4 * c, NZ)


def owner_y(j, c):
    return lax.rem(j + j // 8 + 2 * c, NY)


def owned_at(z, y, c):
    v = lax.rem(z + NZ - 4 * c, NZ)
    first = owner_y(v, c) == y
    second = jnp.logical_and(v < 3, owner_y(v + 8, c) == y)
    return jnp.minimum(jnp.where(first, v, v + 8), HALF - 1), jnp.logical_or(first, second)


def candidates(axis, d, z, y, c):
    if axis == 0:
        u = lax.rem(z + d + NZ - 4 * c, NZ)
        return [(u, None), (jnp.minimum(u + 8, HALF - 1), u < 3)]
    u = lax.rem(y + d + NY - 2 * c, NY)
    return [(u, None), (u + 4, None), (jnp.minimum(u + 7, HALF - 1), u >= 1)]


def guarded(valid, body):
    if valid is None:
        body()
    else:
        pl.when(valid)(body)


Z_UP, Z_DOWN, Y_UP, Y_DOWN, Z_UP_TWO, Z_DOWN_TWO, Y_UP_TWO = range(7)
FAR = 4


def roles(phase, axis, d):
    n = NZ if axis == 0 else NY
    far = n // 2
    up, down = 2 * axis, 2 * axis + 1
    if phase == 2 and axis == 1:
        if d == 0:
            return [(up, None), (down, None), (FAR, None)], []
        if d == far:
            return [], [(Y_UP_TWO, FAR, None)]
        return [], [(up, up, None) if d < far else (down, down, None)]
    receives, sends = [], []
    if d < far - 1:
        receives.append((up, None))
    if d == 0 or d > far + 1:
        receives.append((down, None))
    if phase == 1:
        if d == far - 1:
            receives.append((up, 0))
        if d == far + 1:
            receives.append((down, 1))
    else:
        if d == far - 2:
            receives.append((down, 0))
        if d == far + 2:
            receives.append((up, 1))
    if 1 <= d < far:
        sends.append((up, up, None))
    if d == far and phase == 1:
        sends += [(up, up, 0), (down, down, 1)]
    if d == far and phase == 2:
        sends += [(Z_UP_TWO, down, 0), (Z_DOWN_TWO, up, 1)]
    if d > far:
        sends.append((down, down, None))
    return receives, sends


ORDER = (
    (1, 0, 4, 0), (1, 1, 2, 0),
    (1, 0, 3, 1), (1, 0, 5, 1), (1, 1, 1, 1), (1, 1, 3, 1),
    (1, 0, 2, 2), (1, 0, 6, 2), (1, 1, 0, 2), (2, 0, 4, 2), (2, 0, 3, 2), (2, 0, 5, 2),
    (1, 0, 1, 3), (1, 0, 7, 3), (2, 0, 2, 3), (2, 0, 6, 3),
    (1, 0, 0, 4), (2, 1, 2, 4), (2, 1, 1, 4), (2, 1, 3, 4), (2, 0, 1, 4), (2, 0, 7, 4),
    (2, 1, 0, 5), (2, 0, 0, 5),
)
LAG = 5


def kernel(
    grads, momentum, weights, out, own, other, box, shares, window, near, current, last, scaled, flat, pieces, got, wide,
    load_sem, cross_send, cross_recv, send_sem, recv_sem, share_sem, near_sem, piece_send, piece_recv,
):
    section = lax.axis_index("section")
    me = lax.axis_index("dp")
    z, y, c = place(me)
    mine, is_owner = owned_at(z, y, c)
    is_guest = jnp.logical_not(is_owner)

    def device(nz, ny, nc):
        return (section, (nz * NY + ny) * 2 + nc)

    targets = (
        device(lax.rem(z + 1, NZ), y, c),
        device(lax.rem(z + NZ - 1, NZ), y, c),
        device(z, lax.rem(y + 1, NY), c),
        device(z, lax.rem(y + NY - 1, NY), c),
        device(lax.rem(z + 2, NZ), y, c),
        device(lax.rem(z + NZ - 2, NZ), y, c),
        device(z, lax.rem(y + 2, NY), c),
    )
    partner = device(z, y, 1 - c)

    def rows(k):
        return pl.ds(pl.multiple_of(ROWS * k, 16), ROWS)

    def load(k):
        return pltpu.make_async_copy(
            grads.at[pl.ds(HALF * c, HALF), rows(k)], own.at[:, rows(k)], load_sem.at[k]
        )

    def cross(k):
        return pltpu.make_async_remote_copy(
            src_ref=grads.at[pl.ds(HALF * (1 - c), HALF), rows(k)],
            dst_ref=other.at[:, rows(k)],
            send_sem=cross_send.at[k],
            recv_sem=cross_recv.at[k],
            device_id=partner,
            device_id_type=MESH,
        )

    def hop(j, k, t, target, way):
        part = (rows(k), pl.ds(LOW[t], WIDTH[t]))
        return pltpu.make_async_remote_copy(
            src_ref=own.at[j, part[0], part[1]],
            dst_ref=near.at[part[0], :] if way == FAR else box.at[way, j, part[0], part[1]],
            send_sem=send_sem,
            recv_sem=near_sem.at[k] if way == FAR else recv_sem.at[way, k, j, t],
            device_id=targets[target],
            device_id_type=MESH,
        )

    for k in range(ROUNDS):
        load(k).start()

    barrier = pltpu.get_barrier_semaphore()
    for target in targets[:4] + (partner,):
        pl.semaphore_signal(barrier, inc=1, device_id=target, device_id_type=MESH)

    window[...] = jnp.zeros_like(window)
    shares[c, 0:MATRICES, :] = momentum[...].astype(F32)

    pl.semaphore_wait(barrier, 5)

    exchange = pltpu.make_async_remote_copy(
        src_ref=shares.at[c],
        dst_ref=shares.at[c],
        send_sem=share_sem.at[0],
        recv_sem=share_sem.at[1],
        device_id=partner,
        device_id_type=MESH,
    )
    exchange.start()
    for k in range(ROUNDS):
        cross(k).start()

    line = 9 * (me // 2)
    base = jnp.minimum(16 * (line // 16), HEIGHT - WINDOW)
    shift = line - base
    exchange.wait()
    for core in range(2):

        @pl.when(c == core)
        def _():
            for source in range(2):
                for k in range(STRIPS):
                    at = STRIPS * source + k
                    window[at % 8, pl.ds(shift + at // 8, HALF, stride=WINDOW), :] = shares[
                        source, HALF * core : HALF * (core + 1), 128 * k : 128 * (k + 1)
                    ]

    scale = MOMENTUM_DECAY * MOMENTUM_DECAY / (1.0 + MOMENTUM_DECAY)

    def combine(k):
        load(k).wait()
        cross(k).wait_recv()

        def add(j, carry):
            own[j, rows(k), :] = (
                own[j, rows(k), :] + other[j, rows(k), :]
            )
            return carry

        lax.fori_loop(0, HALF, add, 0)
        for part in range(WINDOW // 16):
            top = base + 16 * part

            @pl.when(top // ROWS == k)
            def _():
                r = pl.ds(pl.multiple_of(top, 16), 16)

                def blend(j, carry):
                    from_window = pl.ds(pl.multiple_of(WINDOW * j + 16 * part, 16), 16)
                    for block in range(8):
                        lanes = pl.ds(128 * block, 128)
                        own[j, r, lanes] = (
                            own[j, r, lanes].astype(F32) + scale * window[block, from_window, :]
                        ).astype(BF16)
                    return carry

                lax.fori_loop(0, HALF, blend, 0)

    steps = []
    for phase, axis, d, lag in ORDER:
        if phase == 1:
            found = candidates(axis, d, z, y, c)
        elif axis == 0:
            found = [owned_at(lax.rem(z + d, NZ), y, c)]
        else:
            found = [owned_at(z, lax.rem(y + d, NY), c)]
        for j, valid in found:
            steps.append((axis if phase == 1 else 1 - axis, j, valid, lag, *roles(phase, axis, d)))

    def step(k, parity, t, j, receives, sends):
        part = (rows(k), pl.ds(LOW[t], WIDTH[t]))

        def take(ways):
            for way in ways:
                hop(j, k, t, 0, way).wait_recv()
            total = own[j, part[0], part[1]].astype(F32)
            for way in ways:
                if way == FAR:
                    total = total + near[part[0], :].astype(F32)
                else:
                    total = total + box[way, j, part[0], part[1]].astype(F32)
            own[j, part[0], part[1]] = total.astype(BF16)

        always = [way for way, when in receives if when is None]
        if always:
            take(always)
        for way, when in receives:
            if when is not None:
                pl.when(parity == when)(lambda way=way: take([way]))
        for target, way, when in sends:
            guarded(
                None if when is None else parity == when,
                lambda target=target, way=way: hop(j, k, t, target, way).start(),
            )

    combine(0)

    def body(i, carry):
        for t, j, valid, lag, receives, sends in steps:
            k = i - lag
            live = jnp.logical_and(k >= 0, k < ROUNDS)
            if valid is not None:
                live = jnp.logical_and(live, valid)
            pl.when(live)(
                lambda k=k, t=t, j=j, receives=receives, sends=sends: step(
                    k, lax.rem(k + c, 2), t, j, receives, sends
                )
            )

        @pl.when(i + 1 < ROUNDS)
        def _():
            combine(i + 1)

        return carry

    lax.fori_loop(0, ROUNDS + LAG, body, 0)

    slot = HALF * c + mine

    def share(to):
        return pltpu.make_async_remote_copy(
            src_ref=pieces.at[to],
            dst_ref=got.at[slot],
            send_sem=piece_send,
            recv_sem=piece_recv,
            device_id=(section, to),
            device_id_type=MESH,
        )

    @pl.when(is_owner)
    def _():
        blended = (1.0 + MOMENTUM_DECAY) * own[mine].astype(F32)
        norm = jnp.sqrt(jnp.sum(blended * blended, keepdims=True)) + EPSILON
        current[...] = (blended / norm).astype(BF16)

        def newton(_, carry):
            x = current[...]
            gram = lax.dot_general(
                x, x, (((1,), (1,)), ((), ())), preferred_element_type=F32
            ).astype(BF16)
            square = jnp.dot(gram, gram, preferred_element_type=F32)
            polynomial = (QUINTIC_B * gram.astype(F32) + QUINTIC_C * square).astype(BF16)
            mixed = jnp.dot(polynomial, x, preferred_element_type=F32)
            current[...] = (QUINTIC_A * x.astype(F32) + mixed).astype(BF16)
            return carry

        lax.fori_loop(0, ITERS - 1, newton, 0)
        x = current[...]
        gram = lax.dot_general(
            x, x, (((1,), (1,)), ((), ())), preferred_element_type=F32
        ).astype(BF16)
        square = jnp.dot(gram, gram, preferred_element_type=F32)
        last[...] = QUINTIC_B * gram.astype(F32) + QUINTIC_C * square
        scaled[...] = QUINTIC_A * x.astype(F32)

        def quarter(i, carry):
            ahead = jnp.where(i == 0, 2, jnp.where(i == 1, 1, jnp.where(i == 2, 3, 0)))
            q = lax.rem(z // 2 + ahead, 4)
            r = pl.ds(pl.multiple_of(QUARTER * q, 8), QUARTER)
            mixed = jnp.dot(last[r, :].astype(BF16), current[...], preferred_element_type=F32)
            new = scaled[r, :] + mixed
            for k in range(8):
                flat[pl.ds(k, QUARTER, stride=8), :] = new[:, 128 * k : 128 * (k + 1)]
            pad = jnp.zeros((STRIP_ROWS - STRIPS, 128), F32)
            for pair in range(8):
                both = flat[2 * STRIPS * pair : 2 * STRIPS * (pair + 1), :]
                to = 16 * q + 2 * pair
                pieces[to] = jnp.concatenate([both[:STRIPS], pad]).astype(BF16)
                pieces[to + 1] = jnp.concatenate([both[STRIPS:], pad]).astype(BF16)

            def send(e, carry):
                to = 16 * q + e

                @pl.when(to != me)
                def _():
                    share(to).start()

                return carry

            lax.fori_loop(0, 16, send, 0, unroll=True)
            return carry

        lax.fori_loop(0, 4, quarter, 0)
        got[slot] = pieces[me]

    for k in range(ROUNDS):
        cross(k).wait_send()

    def sent(number):
        pltpu.make_async_copy(own.at[pl.ds(0, number)], own.at[pl.ds(0, number)], send_sem).wait()

    def arrived(number):
        pltpu.make_async_copy(
            got.at[pl.ds(0, number)], got.at[pl.ds(0, number)], piece_recv
        ).wait()

    @pl.when(is_owner)
    def _():
        sent(HALF - 1)
        arrived(MATRICES - 1)

    @pl.when(is_guest)
    def _():
        sent(HALF)
        arrived(MATRICES)

    for m in range(MATRICES):
        wide[STRIP_ROWS * m : STRIP_ROWS * (m + 1), :] = got[m].astype(F32)
    factor = 0.2 * math.sqrt(max(HEIGHT, BREADTH))
    for k in range(STRIPS):
        lanes = slice(128 * k, 128 * (k + 1))
        update = wide[pl.ds(k, MATRICES, stride=STRIP_ROWS), :]
        out[:, lanes] = (
            weights[:, lanes].astype(F32) * (1.0 - LEARN_RATE * DECAY_RATE)
            - LEARN_RATE * factor * update
        ).astype(BF16)

    @pl.when(is_owner)
    def _():
        pltpu.make_async_copy(
            pieces.at[pl.ds(0, GROUPS - 1)], pieces.at[pl.ds(0, GROUPS - 1)], piece_send
        ).wait()


def local(grads, momentum, weights):
    matrix = (HALF, HEIGHT, BREADTH)
    dma = pltpu.SemaphoreType.DMA
    return pl.pallas_call(
        kernel,
        out_shape=jax.ShapeDtypeStruct((MATRICES, PORTION), BF16),
        in_specs=[pl.BlockSpec(memory_space=pl.ANY)] + [pl.BlockSpec(memory_space=pltpu.VMEM)] * 2,
        out_specs=pl.BlockSpec(memory_space=pltpu.VMEM),
        scratch_shapes=[
            pltpu.VMEM(matrix, BF16),
            pltpu.VMEM(matrix, BF16),
            pltpu.VMEM((4, *matrix), BF16),
            pltpu.VMEM((2, 24, PORTION), F32),
            pltpu.VMEM((8, HALF * WINDOW, 128), F32),
            pltpu.VMEM((HEIGHT, WIDTH[0]), BF16),
            pltpu.VMEM((HEIGHT, BREADTH), BF16),
            pltpu.VMEM((HEIGHT, HEIGHT), F32),
            pltpu.VMEM((HEIGHT, BREADTH), F32),
            pltpu.VMEM((QUARTER * 8, 128), F32),
            pltpu.VMEM((GROUPS, STRIP_ROWS, 128), BF16),
            pltpu.VMEM((MATRICES, STRIP_ROWS, 128), BF16),
            pltpu.VMEM((MATRICES * STRIP_ROWS, 128), F32),
            dma((ROUNDS,)),
            dma((ROUNDS,)),
            dma((ROUNDS,)),
            dma,
            dma((4, ROUNDS, HALF, 2)),
            dma((2,)),
            dma((ROUNDS,)),
            dma,
            dma,
        ],
        compiler_params=pltpu.CompilerParams(
            collective_id=0, has_side_effects=True, vmem_limit_bytes=56 << 20
        ),
        name="muon_step",
    )(grads[0, 0], momentum[0], weights[0])[None]


def solution(mesh):
    placed = (
        P("section", "dp", None, None, None),
        P("section", None, "dp"),
        P("section", None, "dp"),
    )
    return jax.shard_map(
        local, mesh=mesh, in_specs=placed, out_specs=P("section", None, "dp"), check_vma=False
    )
```
